32 devices in a mesh: grp: 2 (over x), row: 8 (over z, y), case: 2 (over core).
Axes of the slice: x: 2, y: 2, z: 4, core: 2. Of those that a mesh axis runs over, the one named last changes fastest.
Arguments:
- cotangent: float32 [768, 8192], P(('grp', 'case'), 'row'), parts along dimension 0, may hold values from -6 to 6
- rotor_index: int32 [768], P(('grp', 'case')), parts along dimension 0, may hold values from 0 to 127
- current_index: int32 [768], P(('grp', 'case')), parts along dimension 0, may hold values from 0 to 15
- position_table: float32 [256, 8192], P('grp', 'row'), parts along dimension 0, may hold values from -6 to 6
- current_table: float32 [32, 8192], P('grp', 'row'), parts along dimension 0, may hold values from -6 to 6
- segment_one: int32 [16384], P(('grp', 'row')), parts along dimension 0, may hold values from 0 to 63
- gain_one: float32 [128], P('grp'), parts along dimension 0, may hold values from 0.1 to 1.9
- field_one: float32 [768, 8192], P(('grp', 'case'), 'row'), parts along dimension 0, may hold values from -6 to 6
- scatter_one: float32 [16384, 8192], P(('grp', 'row'), 'case'), parts along dimension 0, may hold values from -0.0625 to 0.0625
- segment_zero: int32 [16384], P(('grp', 'case')), parts along dimension 0, may hold values from 0 to 63
- gain_zero: float32 [128], P('grp'), parts along dimension 0, may hold values from 0.1 to 1.9
- field_zero: float32 [768, 8192], P(('grp', 'row'), 'case'), parts along dimension 0, may hold values from -6 to 6
- scatter_zero: float32 [16384, 8192], P(('grp', 'case'), 'row'), parts along dimension 0, may hold values from -0.0625 to 0.0625
Outputs:
- adjoint_zero: float32 [768, 8192], P(('grp', 'case'), 'row'), parts along dimension 0
- grad_one: float32 [128], P('grp'), parts along dimension 0
- grad_zero: float32 [128], P('grp'), parts along dimension 0
The draws below stay inside these ranges and needn't reach their ends.
There are 2 independent parts, one for each index of `grp`. The reference program is written for one: setup_inputs(seed, part) draws one part's arguments, and reference() takes and returns one part's arrays. A program takes and returns all parts, laid end to end along the dimension named above; each array names one. Nothing has to cross between parts.
All inputs are finite; a program needn't handle non-finite values.
Results may differ from the reference program's by a relative error of at most 0.00011.
Values sent between devices are 32-bit elements; how exact they have to be, the bound alone decides.
A program may use at most 128 MiB of HBM per device.

```python
import jax
import jax.numpy as jnp
from jax import lax

M = 8192
CASES = 384
POSITIONS = 128
CURRENTS = 16
SEGMENTS = 64


def plant(values, stream_key, smallest, high):
    extent = values.shape
    index_at = [jax.random.randint(jax.random.fold_in(stream_key, axis), (), 0, extent[axis]) for axis in range(len(extent))]
    values = values.at[tuple(index_at)].set(smallest)
    longest = extent.index(max(extent))
    index_at[longest] = (index_at[longest] + 1) % extent[longest]
    return values.at[tuple(index_at)].set(high)


def steps_of(stream_key, shape, pieces, smallest, high):
    factor_of = 1.0
    for axis_at, parts in pieces:
        heights = jax.random.uniform(jax.random.fold_in(jax.random.fold_in(stream_key, 6), axis_at), (parts,), jnp.float32, smallest / len(pieces), high / len(pieces))
        factor_of = factor_of * jnp.repeat(jnp.exp(heights), shape[axis_at] // parts).reshape((-1,) + (1,) * (len(shape) - 1 - axis_at))
    return factor_of


def bell_draw(key, extent, scale, bound, cuts=(), kind=jnp.bfloat16):
    entries = jax.random.normal(key, extent, jnp.float32) * scale
    if len(cuts) > 0:
        entries = steps_of(key, extent, cuts, -0.22, 0.18) * entries
    return jnp.clip(entries, min=-bound, max=bound).astype(kind)


def setup_inputs(seed: int = 0, part: int = 0) -> dict:
    seeds = jax.random.split(jax.random.key(seed), 14)
    part_keys = jax.random.split(jax.random.fold_in(seeds[13], part), 14)
    return {
        "cotangent": bell_draw(part_keys[0], (CASES, M), 1.0, 6.0, ((0, 2), (1, 8)), jnp.float32),
        "rotor_index": plant(jax.random.randint(part_keys[1], (CASES,), 0, POSITIONS), jax.random.fold_in(part_keys[1], 1), 0, POSITIONS - 1).astype(jnp.int32),
        "current_index": plant(jax.random.randint(part_keys[2], (CASES,), 0, CURRENTS), jax.random.fold_in(part_keys[2], 1), 0, CURRENTS - 1).astype(jnp.int32),
        "position_table": bell_draw(part_keys[3], (POSITIONS, M), 1.0, 6.0, ((1, 8),), jnp.float32),
        "current_table": bell_draw(part_keys[4], (CURRENTS, M), 1.0, 6.0, ((1, 8),), jnp.float32),
        "segment_one": plant(jax.random.randint(part_keys[5], (M,), 0, SEGMENTS), jax.random.fold_in(part_keys[5], 1), 0, SEGMENTS - 1).astype(jnp.int32),
        "gain_one": jnp.clip(1.0 + 0.18 * jax.random.normal(part_keys[6], (SEGMENTS,), jnp.float32), 0.1, 1.9),
        "field_one": bell_draw(part_keys[7], (CASES, M), 1.0, 6.0, ((0, 2), (1, 8)), jnp.float32),
        "scatter_one": bell_draw(part_keys[8], (M, M), M ** -0.5, 0.0625, ((0, 8), (1, 2)), jnp.float32),
        "segment_zero": plant(jax.random.randint(part_keys[9], (M,), 0, SEGMENTS), jax.random.fold_in(part_keys[9], 1), 0, SEGMENTS - 1).astype(jnp.int32),
        "gain_zero": jnp.clip(1.0 + 0.18 * jax.random.normal(part_keys[10], (SEGMENTS,), jnp.float32), 0.1, 1.9),
        "field_zero": bell_draw(part_keys[11], (CASES, M), 1.0, 6.0, ((0, 8), (1, 2)), jnp.float32),
        "scatter_zero": bell_draw(part_keys[12], (M, M), M ** -0.5, 0.0625, ((0, 2), (1, 8)), jnp.float32),
    }


def reference(cotangent, rotor_index, current_index, position_table, current_table, segment_one, gain_one, field_one, scatter_one, segment_zero, gain_zero, field_zero, scatter_zero):
    highest = lax.Precision.HIGHEST
    adjoint_seed = cotangent + position_table[rotor_index] + current_table[current_index]
    scaled_two = adjoint_seed * gain_one[segment_one][None, :]
    grad_one = jax.ops.segment_sum(jnp.sum(adjoint_seed * field_one, axis=0), segment_one, num_segments=SEGMENTS) / CASES
    adjoint_one = jnp.dot(scaled_two, scatter_one, precision=highest, preferred_element_type=jnp.float32)
    grad_zero = jax.ops.segment_sum(jnp.sum(adjoint_one * field_zero, axis=0), segment_zero, num_segments=SEGMENTS) / CASES
    scaled_one = adjoint_one * gain_zero[segment_zero][None, :]
    adjoint_zero = jnp.dot(scaled_one, scatter_zero, precision=highest, preferred_element_type=jnp.float32)
    return adjoint_zero, grad_one, grad_zero
```

```python
import functools

import jax
import jax.numpy as jnp
from jax import lax
from jax.experimental import pallas as pl
from jax.experimental.pallas import tpu as pltpu
from jax.sharding import PartitionSpec as P

MESH = pl.DeviceIdType.MESH
LANES = 128
SUBS = 2


def lookup(which, lookup_table):
    onehot = (which[:, None] == jnp.arange(lookup_table.shape[0], dtype=jnp.int32)[None, :]).astype(
        jnp.float32
    )
    return jnp.dot(
        onehot, lookup_table, precision=lax.Precision.HIGHEST, preferred_element_type=jnp.float32
    )


def segment_rows(segment, gains):
    onehot = (segment[:, None] == jnp.arange(gains.shape[0], dtype=jnp.int32)[None, :]).astype(
        jnp.float32
    )
    return jnp.dot(
        onehot, gains, precision=lax.Precision.HIGHEST, preferred_element_type=jnp.float32
    )


def segment_total(values, segment, num_segments):
    onehot = (segment[:, None] == jnp.arange(num_segments, dtype=jnp.int32)[None, :]).astype(
        jnp.float32
    )
    return jnp.dot(
        values, onehot, precision=lax.Precision.HIGHEST, preferred_element_type=jnp.float32
    )


def split(x):
    high = x.astype(jnp.bfloat16)
    return high, (x - high.astype(jnp.float32)).astype(jnp.bfloat16)


def dot3(a_high, a_low, b_high, b_low):
    dot = functools.partial(jnp.dot, preferred_element_type=jnp.float32)
    return dot(a_low, b_high) + dot(a_high, b_low) + dot(a_high, b_high)


def ring_kernel(
    n, cot, rot, cur, ptab, ctab, seg1, gain1, f1, s1, seg0, gain0, f0, s0,
    out, g1_out, g0_out,
    own, peer, a_high, a_low, s1_buf, s0_buf, ring, part, total, other, g0,
    send_sem, recv_sem, s1_sem, s0_sem, pair_send, pair_recv,
):
    row, case = lax.axis_index("row"), lax.axis_index("case")
    half = n // 2
    upper = lax.rem(row, 2)
    place = (row // 2) * (1 - upper) + (n - 1 - row // 2) * upper

    def row_at(position):
        position = lax.rem(position + n, n)
        far = position // half
        return (1 - far) * 2 * position + far * (2 * (n - 1 - position) + 1)

    right, left = row_at(place + 1), row_at(place - 1)
    targets = (right, left)
    local_cases = cot.shape[0]
    cases = 2 * local_cases
    width = ring.shape[3]
    sub = cases // SUBS
    field_cases = f0.shape[0]
    segments = gain1.shape[0]

    def chunk(step, d):
        c = lax.rem(place + 2 * n - step, n) if d == 0 else lax.rem(place + step, n)
        return 2 * c + d

    def second_chunk(t, d):
        return chunk(t + n - 1, d)

    def s1_copy(step, d):
        start = pl.multiple_of(chunk(step, d) * width, width)
        return pltpu.make_async_copy(
            s1.at[:, pl.ds(start, width)], s1_buf.at[2 * step + d], s1_sem.at[2 * step + d]
        )

    def s0_copy(t, d):
        start = pl.multiple_of(second_chunk(t, d) * width, width)
        return pltpu.make_async_copy(
            s0.at[pl.ds(start, width)], s0_buf.at[2 * t + d], s0_sem.at[2 * t + d]
        )

    def ring_copy(step, d, h):
        rows = pl.ds(h * sub, sub)
        return pltpu.make_async_remote_copy(
            src_ref=ring.at[step, d, rows],
            dst_ref=ring.at[step + 1, d, rows],
            send_sem=send_sem.at[step, d, h],
            recv_sem=recv_sem.at[step + 1, d, h],
            device_id={"row": targets[d]},
            device_id_type=MESH,
        )

    def pair_copy(src, dst, at):
        return pltpu.make_async_remote_copy(
            src_ref=src,
            dst_ref=dst,
            send_sem=pair_send.at[at],
            recv_sem=pair_recv.at[at],
            device_id={"case": 1 - case},
            device_id_type=MESH,
        )

    barrier = pltpu.get_barrier_semaphore()
    pl.semaphore_signal(barrier, inc=1, device_id={"row": left}, device_id_type=MESH)
    pl.semaphore_signal(barrier, inc=1, device_id={"row": right}, device_id_type=MESH)
    pl.semaphore_signal(barrier, inc=1, device_id={"case": 1 - case}, device_id_type=MESH)

    for step in range(n):
        for d in range(2):
            s1_copy(step, d).start()

    highest = functools.partial(
        jnp.dot, precision=lax.Precision.HIGHEST, preferred_element_type=jnp.float32
    )

    def pick(index, count):
        ids = lax.broadcasted_iota(jnp.int32, (local_cases, count), 1)
        return jnp.where(ids == index, 1.0, 0.0).astype(jnp.float32)

    def members(segment):
        return lax.broadcasted_iota(jnp.int32, (segments, segment.shape[1]), 0) == segment

    def gain_row(segment, gains):
        return jnp.sum(jnp.where(members(segment), gains, 0.0), axis=0, keepdims=True)

    def fold(values):
        folded = values[:, :LANES]
        for at in range(LANES, values.shape[1], LANES):
            folded = folded + values[:, at : at + LANES]
        return folded

    seed = (
        cot[...]
        + highest(pick(rot[...], ptab.shape[0]), ptab[...])
        + highest(pick(cur[...], ctab.shape[0]), ctab[...])
    )
    own[...] = seed * gain_row(seg1[...], gain1[...])
    pl.semaphore_wait(barrier, 3)
    pair_copy(own, peer, 0).start()
    mine = pl.ds(pl.multiple_of(case * local_cases, local_cases), local_cases)
    theirs = pl.ds(pl.multiple_of((1 - case) * local_cases, local_cases), local_cases)
    a_high[mine], a_low[mine] = split(own[...])
    column = jnp.sum(seed * f1[...], axis=0, keepdims=True)
    picked = fold(jnp.where(members(seg1[...]), column, 0.0))
    g1_out[...] = jnp.sum(picked, axis=1, keepdims=True)
    g0[...] = jnp.zeros_like(g0)
    total[...] = jnp.zeros_like(total)
    pair_copy(own, peer, 0).wait_recv()
    a_high[theirs], a_low[theirs] = split(peer[...])

    def product(step, d):
        s1_copy(step, d).wait()
        b_high, b_low = split(s1_buf[2 * step + d])
        return dot3(a_high[...], a_low[...], b_high, b_low)

    for d in range(2):
        ring[0, d] = product(0, d)
        for h in range(SUBS):
            ring_copy(0, d, h).start()
    for t in range(n):
        for d in range(2):
            s0_copy(t, d).start()

    def reduce_step(step, carry):
        for d in range(2):
            part[d] = product(step, d)
        for h in range(SUBS):
            for d in range(2):
                rows = pl.ds(h * sub, sub)
                ring_copy(step - 1, d, h).wait_recv()
                ring[step, d, rows] = ring[step, d, rows] + part[d, rows]
                ring_copy(step, d, h).start()
        return carry

    lax.fori_loop(1, n, reduce_step, 0)

    def second(t, rows):
        for d in range(2):
            start = pl.multiple_of(second_chunk(t, d) * width, width)
            segment = seg0[:, pl.ds(start, width)]
            x_high, x_low = split(ring[n - 1 + t, d, rows] * gain_row(segment, gain0[...]))
            b_high, b_low = split(s0_buf[2 * t + d])
            total[rows] = total[rows] + dot3(x_high, x_low, b_high, b_low)

    def gradient(t):
        for d in range(2):
            start = pl.multiple_of(second_chunk(t, d) * width, width)
            segment = seg0[:, pl.ds(start, width)]
            at = pl.multiple_of(row * field_cases, 8)
            column = jnp.sum(
                ring[n - 1 + t, d, pl.ds(at, field_cases)] * f0[:, pl.ds(start, width)],
                axis=0,
                keepdims=True,
            )
            g0[...] = g0[...] + fold(jnp.where(members(segment), column, 0.0))

    def gather_step(t, carry):
        for d in range(2):
            s0_copy(t, d).wait()
        second(t, pl.ds(0, cases))
        gradient(t)
        step = n + t
        for h in range(SUBS):
            for d in range(2):
                ring_copy(step - 1, d, h).wait_recv()

                @pl.when(t < n - 2)
                def _():
                    ring_copy(step, d, h).start()

        return carry

    lax.fori_loop(0, n - 1, gather_step, 0)
    for d in range(2):
        s0_copy(n - 1, d).wait()
    second(n - 1, theirs)
    pair_copy(total.at[theirs], other, 1).start()
    second(n - 1, mine)
    gradient(n - 1)
    g0_out[...] = jnp.sum(g0[...], axis=1, keepdims=True)
    pair_copy(total.at[theirs], other, 1).wait_recv()
    out[...] = total[mine] + other[...]

    pair_copy(own, peer, 0).wait_send()
    pair_copy(total.at[theirs], other, 1).wait_send()

    def drain(step, carry):
        for d in range(2):
            for h in range(SUBS):
                ring_copy(step, d, h).wait_send()
        return carry

    lax.fori_loop(0, 2 * n - 2, drain, 0)


def ring_call(n, args):
    (cot, rot, cur, ptab, ctab, seg1, gain1, f1, s1, seg0, gain0, f0, s0) = args
    local_cases, depth = cot.shape
    cases = 2 * local_cases
    columns = s1.shape[1]
    width = columns // (2 * n)
    segments = gain1.shape[0]
    vmem = pl.BlockSpec(memory_space=pltpu.VMEM)
    hbm = pl.BlockSpec(memory_space=pl.ANY)
    f32, bf16 = jnp.float32, jnp.bfloat16
    dma = pltpu.SemaphoreType.DMA
    return pl.pallas_call(
        functools.partial(ring_kernel, n),
        out_shape=(
            jax.ShapeDtypeStruct((local_cases, depth), f32),
            jax.ShapeDtypeStruct((segments, 1), f32),
            jax.ShapeDtypeStruct((segments, 1), f32),
        ),
        in_specs=[vmem] * 8 + [hbm] + [vmem] * 3 + [hbm],
        out_specs=(vmem, vmem, vmem),
        scratch_shapes=[
            pltpu.VMEM((local_cases, depth), f32),
            pltpu.VMEM((local_cases, depth), f32),
            pltpu.VMEM((cases, depth), bf16),
            pltpu.VMEM((cases, depth), bf16),
            pltpu.VMEM((2 * n, depth, width), f32),
            pltpu.VMEM((2 * n, width, depth), f32),
            pltpu.VMEM((2 * n - 1, 2, cases, width), f32),
            pltpu.VMEM((2, cases, width), f32),
            pltpu.VMEM((cases, depth), f32),
            pltpu.VMEM((local_cases, depth), f32),
            pltpu.VMEM((segments, LANES), f32),
            dma((2 * n - 1, 2, SUBS)),
            dma((2 * n - 1, 2, SUBS)),
            dma((2 * n,)),
            dma((2 * n,)),
            dma((2,)),
            dma((2,)),
        ],
        compiler_params=pltpu.CompilerParams(
            collective_id=0, has_side_effects=True, vmem_limit_bytes=62 * 1024 * 1024
        ),
        cost_estimate=pl.CostEstimate(
            flops=12 * cases * depth * columns, bytes_accessed=12 * depth * columns, transcendentals=0
        ),
    )(
        cot, rot[:, None], cur[:, None], ptab, ctab, seg1[None, :], gain1[:, None], f1, s1,
        seg0[None, :], gain0[:, None], f0, s0,
    )


def local(n, *args):
    (cot, rot, cur, ptab, ctab, seg1, gain1, f1, s1, seg0, gain0, f0, s0) = args
    width = s1.shape[1] // (2 * n)
    if n % 2 == 0 and width % LANES == 0 and width * 2 * n == s1.shape[1]:
        adjoint_zero, partial_one, partial_zero = ring_call(n, args)
        partial_one, partial_zero = partial_one[:, 0], partial_zero[:, 0]
        total_cases = 2 * cot.shape[0]
    else:
        highest = lax.Precision.HIGHEST
        num_segments = gain1.shape[0]
        adjoint_seed = cot + lookup(rot, ptab) + lookup(cur, ctab)
        scaled_two = adjoint_seed * segment_rows(seg1, gain1)[None, :]
        partial_one = segment_total(jnp.sum(adjoint_seed * f1, axis=0), seg1, num_segments)
        all_seeds = lax.all_gather(scaled_two, "case", axis=0, tiled=True)
        total_cases = all_seeds.shape[0]
        own_adjoint = lax.psum_scatter(
            jnp.dot(all_seeds, s1, precision=highest, preferred_element_type=jnp.float32),
            "row",
            scatter_dimension=0,
            tiled=True,
        )
        scaled_one = own_adjoint * segment_rows(seg0, gain0)[None, :]
        zero_terms = jnp.dot(
            lax.all_gather(scaled_one, "row", axis=0, tiled=True),
            s0,
            precision=highest,
            preferred_element_type=jnp.float32,
        )
        partial_zero = segment_total(jnp.sum(own_adjoint * f0, axis=0), seg0, num_segments)
        adjoint_zero = lax.psum_scatter(zero_terms, "case", scatter_dimension=0, tiled=True)
    grad_one, grad_zero = lax.psum((partial_one, partial_zero), ("row", "case"))
    return (adjoint_zero, grad_one / total_cases, grad_zero / total_cases)


def solution(mesh):
    placed = (
        P(("grp", "case"), "row"),
        P(("grp", "case")),
        P(("grp", "case")),
        P("grp", "row"),
        P("grp", "row"),
        P(("grp", "row")),
        P("grp"),
        P(("grp", "case"), "row"),
        P(("grp", "row"), "case"),
        P(("grp", "case")),
        P("grp"),
        P(("grp", "row"), "case"),
        P(("grp", "case"), "row"),
    )
    return jax.shard_map(
        functools.partial(local, mesh.shape["row"]),
        mesh=mesh,
        in_specs=placed,
        out_specs=(P(("grp", "case"), "row"), P("grp"), P("grp")),
        check_vma=False,
    )
```

```python
import functools

import jax
import jax.numpy as jnp
from jax import lax
from jax.experimental import pallas as pl
from jax.experimental.pallas import tpu as pltpu
from jax.sharding import PartitionSpec as P

MESH = pl.DeviceIdType.MESH
LANES = 128
SUBS = 4


def lookup(which, lookup_table):
    onehot = (which[:, None] == jnp.arange(lookup_table.shape[0], dtype=jnp.int32)[None, :]).astype(
        jnp.float32
    )
    return jnp.dot(
        onehot, lookup_table, precision=lax.Precision.HIGHEST, preferred_element_type=jnp.float32
    )


def segment_rows(segment, gains):
    onehot = (segment[:, None] == jnp.arange(gains.shape[0], dtype=jnp.int32)[None, :]).astype(
        jnp.float32
    )
    return jnp.dot(
        onehot, gains, precision=lax.Precision.HIGHEST, preferred_element_type=jnp.float32
    )


def segment_total(values, segment, num_segments):
    onehot = (segment[:, None] == jnp.arange(num_segments, dtype=jnp.int32)[None, :]).astype(
        jnp.float32
    )
    return jnp.dot(
        values, onehot, precision=lax.Precision.HIGHEST, preferred_element_type=jnp.float32
    )


def split(x):
    high = x.astype(jnp.bfloat16)
    return high, (x - high.astype(jnp.float32)).astype(jnp.bfloat16)


def dot3(a_high, a_low, b_high, b_low):
    dot = functools.partial(jnp.dot, preferred_element_type=jnp.float32)
    return dot(a_low, b_high) + dot(a_high, b_low) + dot(a_high, b_high)


def ring_kernel(
    n, cot, rot, cur, ptab, ctab, seg1, gain1, f1, s1, seg0, gain0, f0, s0,
    out, g1_out, g0_out,
    own, peer, a_high, a_low, s1_buf, s0_buf, ring, part, total, other, g1, g0, pair_grads, row_grads,
    send_sem, recv_sem, s1_sem, s0_sem, pair_send, pair_recv, row_send, row_recv,
):
    row, case = lax.axis_index("row"), lax.axis_index("case")
    half = n // 2
    upper = lax.rem(row, 2)
    place = (row // 2) * (1 - upper) + (n - 1 - row // 2) * upper

    def row_at(position):
        position = lax.rem(position + n, n)
        far = position // half
        return (1 - far) * 2 * position + far * (2 * (n - 1 - position) + 1)

    right, left = row_at(place + 1), row_at(place - 1)
    targets = (right, left)
    local_cases = cot.shape[0]
    cases = 2 * local_cases
    width = ring.shape[3]
    sub = cases // SUBS
    field_cases = f0.shape[0]
    segments = gain1.shape[1]

    def chunk(step, d):
        c = lax.rem(place + 2 * n - step, n) if d == 0 else lax.rem(place + step, n)
        return 2 * c + d

    def second_chunk(t, d):
        return chunk(t + n - 1, d)

    def s1_copy(step, d):
        start = pl.multiple_of(chunk(step, d) * width, width)
        return pltpu.make_async_copy(
            s1.at[:, pl.ds(start, width)], s1_buf.at[2 * step + d], s1_sem.at[2 * step + d]
        )

    def s0_copy(t, d):
        start = pl.multiple_of(second_chunk(t, d) * width, width)
        return pltpu.make_async_copy(
            s0.at[pl.ds(start, width)], s0_buf.at[2 * t + d], s0_sem.at[2 * t + d]
        )

    def ring_copy(step, d, h):
        rows = pl.ds(h * sub, sub)
        return pltpu.make_async_remote_copy(
            src_ref=ring.at[step, d, rows],
            dst_ref=ring.at[step + 1, d, rows],
            send_sem=send_sem.at[step, d, h],
            recv_sem=recv_sem.at[step + 1, d, h],
            device_id={"row": targets[d]},
            device_id_type=MESH,
        )

    def pair_copy(src, dst, at):
        return pltpu.make_async_remote_copy(
            src_ref=src,
            dst_ref=dst,
            send_sem=pair_send.at[at],
            recv_sem=pair_recv.at[at],
            device_id={"case": 1 - case},
            device_id_type=MESH,
        )

    def row_copy(k):
        return pltpu.make_async_remote_copy(
            src_ref=row_grads.at[row],
            dst_ref=row_grads.at[row],
            send_sem=row_send.at[k],
            recv_sem=row_recv.at[row],
            device_id={"row": lax.rem(row + k, n)},
            device_id_type=MESH,
        )

    def row_arrival(k):
        source = lax.rem(row + k, n)
        return pltpu.make_async_remote_copy(
            src_ref=row_grads.at[source],
            dst_ref=row_grads.at[source],
            send_sem=row_send.at[k],
            recv_sem=row_recv.at[source],
            device_id={"row": source},
            device_id_type=MESH,
        )

    barrier = pltpu.get_barrier_semaphore()
    for k in range(1, n):
        pl.semaphore_signal(
            barrier, inc=1, device_id={"row": lax.rem(row + k, n)}, device_id_type=MESH
        )
    pl.semaphore_signal(barrier, inc=1, device_id={"case": 1 - case}, device_id_type=MESH)

    for step in range(n):
        for d in range(2):
            s1_copy(step, d).start()

    highest = functools.partial(
        jnp.dot, precision=lax.Precision.HIGHEST, preferred_element_type=jnp.float32
    )

    def pick(index, count):
        ids = lax.broadcasted_iota(jnp.int32, (local_cases, count), 1)
        column = upright(index.astype(jnp.float32)).astype(jnp.int32)
        return jnp.where(ids == column, 1.0, 0.0).astype(jnp.float32)

    def diagonal(size):
        down = lax.broadcasted_iota(jnp.int32, (size, size), 0)
        return down == lax.broadcasted_iota(jnp.int32, (size, size), 1)

    def upright(values):
        return jnp.sum(jnp.where(diagonal(values.shape[1]), values, 0.0), axis=1, keepdims=True)

    def flat(values):
        return jnp.sum(jnp.where(diagonal(values.shape[0]), values, 0.0), axis=0, keepdims=True)

    gains_one, gains_zero = upright(gain1[...]), upright(gain0[...])

    def members(segment):
        return lax.broadcasted_iota(jnp.int32, (segments, segment.shape[1]), 0) == segment

    def gain_row(segment, gains):
        return jnp.sum(jnp.where(members(segment), gains, 0.0), axis=0, keepdims=True)

    def fold(values):
        folded = values[:, :LANES]
        for at in range(LANES, values.shape[1], LANES):
            folded = folded + values[:, at : at + LANES]
        return folded

    seed = (
        cot[...]
        + highest(pick(rot[...], ptab.shape[0]), ptab[...])
        + highest(pick(cur[...], ctab.shape[0]), ctab[...])
    )
    own[...] = seed * gain_row(seg1[...], gains_one)
    pl.semaphore_wait(barrier, n)
    pair_copy(own, peer, 0).start()
    mine = pl.ds(pl.multiple_of(case * local_cases, local_cases), local_cases)
    theirs = pl.ds(pl.multiple_of((1 - case) * local_cases, local_cases), local_cases)
    a_high[mine], a_low[mine] = split(own[...])
    column = jnp.sum(seed * f1[...], axis=0, keepdims=True)
    g1[...] = fold(jnp.where(members(seg1[...]), column, 0.0))
    g0[...] = jnp.zeros_like(g0)
    total[...] = jnp.zeros_like(total)
    pair_copy(own, peer, 0).wait_recv()
    a_high[theirs], a_low[theirs] = split(peer[...])

    def product(step, d):
        s1_copy(step, d).wait()
        b_high, b_low = split(s1_buf[2 * step + d])
        return dot3(a_high[...], a_low[...], b_high, b_low)

    for d in range(2):
        ring[0, d] = product(0, d)
        for h in range(SUBS):
            ring_copy(0, d, h).start()
    for t in range(n):
        for d in range(2):
            s0_copy(t, d).start()

    def reduce_step(step, carry):
        for d in range(2):
            part[d] = product(step, d)
        for h in range(SUBS):
            for d in range(2):
                rows = pl.ds(h * sub, sub)
                ring_copy(step - 1, d, h).wait_recv()
                ring[step, d, rows] = ring[step, d, rows] + part[d, rows]
                ring_copy(step, d, h).start()
        return carry

    lax.fori_loop(1, n, reduce_step, 0)

    def second(t, rows):
        for d in range(2):
            start = pl.multiple_of(second_chunk(t, d) * width, width)
            segment = seg0[:, pl.ds(start, width)]
            x_high, x_low = split(ring[n - 1 + t, d, rows] * gain_row(segment, gains_zero))
            b_high, b_low = split(s0_buf[2 * t + d])
            total[rows] = total[rows] + dot3(x_high, x_low, b_high, b_low)

    def gradient(t):
        for d in range(2):
            start = pl.multiple_of(second_chunk(t, d) * width, width)
            segment = seg0[:, pl.ds(start, width)]
            at = pl.multiple_of(row * field_cases, 8)
            column = jnp.sum(
                ring[n - 1 + t, d, pl.ds(at, field_cases)] * f0[:, pl.ds(start, width)],
                axis=0,
                keepdims=True,
            )
            g0[...] = g0[...] + fold(jnp.where(members(segment), column, 0.0))

    def gather_step(t, carry):
        for d in range(2):
            s0_copy(t, d).wait()
        second(t, pl.ds(0, cases))
        gradient(t)
        step = n + t
        for h in range(SUBS):
            for d in range(2):
                ring_copy(step - 1, d, h).wait_recv()

                @pl.when(t < n - 2)
                def _():
                    ring_copy(step, d, h).start()

        return carry

    lax.fori_loop(0, n - 1, gather_step, 0)
    for d in range(2):
        s0_copy(n - 1, d).wait()
    gradient(n - 1)
    pair_grads[0] = jnp.sum(g1[...], axis=1, keepdims=True) + jnp.zeros((segments, LANES), jnp.float32)
    pair_grads[1] = jnp.sum(g0[...], axis=1, keepdims=True) + jnp.zeros((segments, LANES), jnp.float32)
    grad_copy = pair_copy(pair_grads.at[pl.ds(0, 2)], pair_grads.at[pl.ds(2, 2)], 2)
    grad_copy.start()
    second(n - 1, theirs)
    pair_copy(total.at[theirs], other, 1).start()
    grad_copy.wait_recv()
    row_grads[row] = pair_grads[pl.ds(0, 2)] + pair_grads[pl.ds(2, 2)]
    for k in range(1, n):
        row_copy(k).start()
    second(n - 1, mine)
    for k in range(1, n):
        row_arrival(k).wait_recv()
    grads = row_grads[0]
    for k in range(1, n):
        grads = grads + row_grads[k]
    g1_out[...] = flat(grads[0, :, :1]) / cases
    g0_out[...] = flat(grads[1, :, :1]) / cases
    pair_copy(total.at[theirs], other, 1).wait_recv()
    out[...] = total[mine] + other[...]

    pair_copy(own, peer, 0).wait_send()
    pair_copy(total.at[theirs], other, 1).wait_send()
    grad_copy.wait_send()
    for k in range(1, n):
        row_copy(k).wait_send()

    def drain(step, carry):
        for d in range(2):
            for h in range(SUBS):
                ring_copy(step, d, h).wait_send()
        return carry

    lax.fori_loop(0, 2 * n - 2, drain, 0)


def ring_call(n, args):
    (cot, rot, cur, ptab, ctab, seg1, gain1, f1, s1, seg0, gain0, f0, s0) = args
    local_cases, depth = cot.shape
    cases = 2 * local_cases
    columns = s1.shape[1]
    width = columns // (2 * n)
    segments = gain1.shape[0]
    vmem = pl.BlockSpec(memory_space=pltpu.VMEM)
    hbm = pl.BlockSpec(memory_space=pl.ANY)
    f32, bf16 = jnp.float32, jnp.bfloat16
    dma = pltpu.SemaphoreType.DMA
    return pl.pallas_call(
        functools.partial(ring_kernel, n),
        out_shape=(
            jax.ShapeDtypeStruct((local_cases, depth), f32),
            jax.ShapeDtypeStruct((1, segments), f32),
            jax.ShapeDtypeStruct((1, segments), f32),
        ),
        in_specs=[vmem] * 8 + [hbm] + [vmem] * 3 + [hbm],
        out_specs=(vmem, vmem, vmem),
        scratch_shapes=[
            pltpu.VMEM((local_cases, depth), f32),
            pltpu.VMEM((local_cases, depth), f32),
            pltpu.VMEM((cases, depth), bf16),
            pltpu.VMEM((cases, depth), bf16),
            pltpu.VMEM((2 * n, depth, width), f32),
            pltpu.VMEM((2 * n, width, depth), f32),
            pltpu.VMEM((2 * n - 1, 2, cases, width), f32),
            pltpu.VMEM((2, cases, width), f32),
            pltpu.VMEM((cases, depth), f32),
            pltpu.VMEM((local_cases, depth), f32),
            pltpu.VMEM((segments, LANES), f32),
            pltpu.VMEM((segments, LANES), f32),
            pltpu.VMEM((4, segments, LANES), f32),
            pltpu.VMEM((n, 2, segments, LANES), f32),
            dma((2 * n - 1, 2, SUBS)),
            dma((2 * n - 1, 2, SUBS)),
            dma((2 * n,)),
            dma((2 * n,)),
            dma((3,)),
            dma((3,)),
            dma((n,)),
            dma((n,)),
        ],
        compiler_params=pltpu.CompilerParams(
            collective_id=0, has_side_effects=True, vmem_limit_bytes=62 * 1024 * 1024
        ),
        cost_estimate=pl.CostEstimate(
            flops=12 * cases * depth * columns, bytes_accessed=12 * depth * columns, transcendentals=0
        ),
    )(
        cot, rot[None, :], cur[None, :], ptab, ctab, seg1[None, :], gain1[None, :], f1, s1,
        seg0[None, :], gain0[None, :], f0, s0,
    )


def local(n, *args):
    (cot, rot, cur, ptab, ctab, seg1, gain1, f1, s1, seg0, gain0, f0, s0) = args
    width = s1.shape[1] // (2 * n)
    if n % 2 == 0 and width % LANES == 0 and width * 2 * n == s1.shape[1]:
        adjoint_zero, grad_one, grad_zero = ring_call(n, args)
        return adjoint_zero, grad_one[0], grad_zero[0]
    highest = lax.Precision.HIGHEST
    num_segments = gain1.shape[0]
    adjoint_seed = cot + lookup(rot, ptab) + lookup(cur, ctab)
    scaled_two = adjoint_seed * segment_rows(seg1, gain1)[None, :]
    partial_one = segment_total(jnp.sum(adjoint_seed * f1, axis=0), seg1, num_segments)
    all_seeds = lax.all_gather(scaled_two, "case", axis=0, tiled=True)
    total_cases = all_seeds.shape[0]
    own_adjoint = lax.psum_scatter(
        jnp.dot(all_seeds, s1, precision=highest, preferred_element_type=jnp.float32),
        "row",
        scatter_dimension=0,
        tiled=True,
    )
    scaled_one = own_adjoint * segment_rows(seg0, gain0)[None, :]
    zero_terms = jnp.dot(
        lax.all_gather(scaled_one, "row", axis=0, tiled=True),
        s0,
        precision=highest,
        preferred_element_type=jnp.float32,
    )
    partial_zero = segment_total(jnp.sum(own_adjoint * f0, axis=0), seg0, num_segments)
    adjoint_zero = lax.psum_scatter(zero_terms, "case", scatter_dimension=0, tiled=True)
    grad_one, grad_zero = lax.psum((partial_one, partial_zero), ("row", "case"))
    return (adjoint_zero, grad_one / total_cases, grad_zero / total_cases)


def solution(mesh):
    placed = (
        P(("grp", "case"), "row"),
        P(("grp", "case")),
        P(("grp", "case")),
        P("grp", "row"),
        P("grp", "row"),
        P(("grp", "row")),
        P("grp"),
        P(("grp", "case"), "row"),
        P(("grp", "row"), "case"),
        P(("grp", "case")),
        P("grp"),
        P(("grp", "row"), "case"),
        P(("grp", "case"), "row"),
    )
    return jax.shard_map(
        functools.partial(local, mesh.shape["row"]),
        mesh=mesh,
        in_specs=placed,
        out_specs=(P(("grp", "case"), "row"), P("grp"), P("grp")),
        check_vma=False,
    )
```

```python
import functools

import jax
import jax.numpy as jnp
from jax import lax
from jax.experimental import pallas as pl
from jax.experimental.pallas import tpu as pltpu
from jax.sharding import PartitionSpec as P

MESH = pl.DeviceIdType.MESH
LANES = 128
SUBS = 2


def lookup(which, lookup_table):
    onehot = (which[:, None] == jnp.arange(lookup_table.shape[0], dtype=jnp.int32)[None, :]).astype(
        jnp.float32
    )
    return jnp.dot(
        onehot, lookup_table, precision=lax.Precision.HIGHEST, preferred_element_type=jnp.float32
    )


def segment_rows(segment, gains):
    onehot = (segment[:, None] == jnp.arange(gains.shape[0], dtype=jnp.int32)[None, :]).astype(
        jnp.float32
    )
    return jnp.dot(
        onehot, gains, precision=lax.Precision.HIGHEST, preferred_element_type=jnp.float32
    )


def segment_total(values, segment, num_segments):
    onehot = (segment[:, None] == jnp.arange(num_segments, dtype=jnp.int32)[None, :]).astype(
        jnp.float32
    )
    return jnp.dot(
        values, onehot, precision=lax.Precision.HIGHEST, preferred_element_type=jnp.float32
    )


def split(x):
    high = x.astype(jnp.bfloat16)
    return high, (x - high.astype(jnp.float32)).astype(jnp.bfloat16)


def dot3(a_high, a_low, b_high, b_low):
    dot = functools.partial(jnp.dot, preferred_element_type=jnp.float32)
    return dot(a_low, b_high) + dot(a_high, b_low) + dot(a_high, b_high)


def ring_kernel(
    n, cot, rot, cur, ptab, ctab, seg1, gain1, f1, s1, seg0, gain0, f0, s0,
    out, g1_out, g0_out,
    own, peer, a_high, a_low, s1_buf, s0_buf, ring, part, total, other, g1, g0, pair_grads, row_grads,
    send_sem, recv_sem, s1_sem, s0_sem, pair_send, pair_recv, row_send, row_recv,
):
    row, case = lax.axis_index("row"), lax.axis_index("case")
    half = n // 2
    upper = lax.rem(row, 2)
    place = (row // 2) * (1 - upper) + (n - 1 - row // 2) * upper

    def row_at(position):
        position = lax.rem(position + n, n)
        far = position // half
        return (1 - far) * 2 * position + far * (2 * (n - 1 - position) + 1)

    right, left = row_at(place + 1), row_at(place - 1)
    targets = (right, left)
    local_cases = cot.shape[0]
    cases = 2 * local_cases
    width = ring.shape[3]
    sub = cases // SUBS
    field_cases = f0.shape[0]
    segments = gain1.shape[1]

    def chunk(step, d):
        c = lax.rem(place + 2 * n - step, n) if d == 0 else lax.rem(place + step, n)
        return 2 * c + d

    def second_chunk(t, d):
        return chunk(t + n - 1, d)

    def s1_copy(step, d):
        start = pl.multiple_of(chunk(step, d) * width, width)
        return pltpu.make_async_copy(
            s1.at[:, pl.ds(start, width)], s1_buf.at[2 * step + d], s1_sem.at[2 * step + d]
        )

    def s0_copy(t, d):
        start = pl.multiple_of(second_chunk(t, d) * width, width)
        return pltpu.make_async_copy(
            s0.at[pl.ds(start, width)], s0_buf.at[2 * t + d], s0_sem.at[2 * t + d]
        )

    def ring_copy(step, d, h):
        rows = pl.ds(h * sub, sub)
        return pltpu.make_async_remote_copy(
            src_ref=ring.at[step, d, rows],
            dst_ref=ring.at[step + 1, d, rows],
            send_sem=send_sem.at[step, d, h],
            recv_sem=recv_sem.at[step + 1, d, h],
            device_id={"row": targets[d]},
            device_id_type=MESH,
        )

    def pair_copy(src, dst, at):
        return pltpu.make_async_remote_copy(
            src_ref=src,
            dst_ref=dst,
            send_sem=pair_send.at[at],
            recv_sem=pair_recv.at[at],
            device_id={"case": 1 - case},
            device_id_type=MESH,
        )

    def row_copy(k):
        return pltpu.make_async_remote_copy(
            src_ref=row_grads.at[row],
            dst_ref=row_grads.at[row],
            send_sem=row_send.at[k],
            recv_sem=row_recv.at[row],
            device_id={"row": lax.rem(row + k, n)},
            device_id_type=MESH,
        )

    def row_arrival(k):
        source = lax.rem(row + k, n)
        return pltpu.make_async_remote_copy(
            src_ref=row_grads.at[source],
            dst_ref=row_grads.at[source],
            send_sem=row_send.at[k],
            recv_sem=row_recv.at[source],
            device_id={"row": source},
            device_id_type=MESH,
        )

    barrier = pltpu.get_barrier_semaphore()
    for k in range(1, n):
        pl.semaphore_signal(
            barrier, inc=1, device_id={"row": lax.rem(row + k, n)}, device_id_type=MESH
        )
    pl.semaphore_signal(barrier, inc=1, device_id={"case": 1 - case}, device_id_type=MESH)

    for step in range(n):
        for d in range(2):
            s1_copy(step, d).start()

    highest = functools.partial(
        jnp.dot, precision=lax.Precision.HIGHEST, preferred_element_type=jnp.float32
    )

    def pick(index, count):
        ids = lax.broadcasted_iota(jnp.int32, (local_cases, count), 1)
        column = upright(index.astype(jnp.float32)).astype(jnp.int32)
        return jnp.where(ids == column, 1.0, 0.0).astype(jnp.float32)

    def diagonal(size):
        down = lax.broadcasted_iota(jnp.int32, (size, size), 0)
        return down == lax.broadcasted_iota(jnp.int32, (size, size), 1)

    def upright(values):
        return jnp.sum(jnp.where(diagonal(values.shape[1]), values, 0.0), axis=1, keepdims=True)

    def flat(values):
        return jnp.sum(jnp.where(diagonal(values.shape[0]), values, 0.0), axis=0, keepdims=True)

    gains_one, gains_zero = upright(gain1[...]), upright(gain0[...])

    def members(segment):
        return lax.broadcasted_iota(jnp.int32, (segments, segment.shape[1]), 0) == segment

    def gain_row(segment, gains):
        return jnp.sum(jnp.where(members(segment), gains, 0.0), axis=0, keepdims=True)

    def fold(values):
        folded = values[:, :LANES]
        for at in range(LANES, values.shape[1], LANES):
            folded = folded + values[:, at : at + LANES]
        return folded

    seed = (
        cot[...]
        + highest(pick(rot[...], ptab.shape[0]), ptab[...])
        + highest(pick(cur[...], ctab.shape[0]), ctab[...])
    )
    own[...] = seed * gain_row(seg1[...], gains_one)
    pl.semaphore_wait(barrier, n)
    pair_copy(own, peer, 0).start()
    mine = pl.ds(pl.multiple_of(case * local_cases, local_cases), local_cases)
    theirs = pl.ds(pl.multiple_of((1 - case) * local_cases, local_cases), local_cases)
    a_high[mine], a_low[mine] = split(own[...])
    column = jnp.sum(seed * f1[...], axis=0, keepdims=True)
    g1[...] = fold(jnp.where(members(seg1[...]), column, 0.0))
    g0[...] = jnp.zeros_like(g0)
    total[...] = jnp.zeros_like(total)
    pair_copy(own, peer, 0).wait_recv()
    a_high[theirs], a_low[theirs] = split(peer[...])

    def product(step, d):
        s1_copy(step, d).wait()
        b_high, b_low = split(s1_buf[2 * step + d])
        return dot3(a_high[...], a_low[...], b_high, b_low)

    for d in range(2):
        ring[0, d] = product(0, d)
        for h in range(SUBS):
            ring_copy(0, d, h).start()
    for t in range(n):
        for d in range(2):
            s0_copy(t, d).start()

    def reduce_step(step, carry):
        now = lax.rem(step, 2)
        for h in range(SUBS):
            for d in range(2):
                rows = pl.ds(h * sub, sub)
                ring_copy(step - 1, d, h).wait_recv()
                ring[step, d, rows] = ring[step, d, rows] + part[now, d, rows]
                ring_copy(step, d, h).start()

            @pl.when(step < n - 1)
            def _():
                part[1 - now, h] = product(step + 1, h)

        return carry

    for d in range(2):
        part[1, d] = product(1, d)

    lax.fori_loop(1, n, reduce_step, 0)

    def second(t, rows, directions=(0, 1)):
        for d in directions:
            start = pl.multiple_of(second_chunk(t, d) * width, width)
            segment = seg0[:, pl.ds(start, width)]
            x_high, x_low = split(ring[n - 1 + t, d, rows] * gain_row(segment, gains_zero))
            b_high, b_low = split(s0_buf[2 * t + d])
            total[rows] = total[rows] + dot3(x_high, x_low, b_high, b_low)

    def gradient(t):
        for d in range(2):
            start = pl.multiple_of(second_chunk(t, d) * width, width)
            segment = seg0[:, pl.ds(start, width)]
            at = pl.multiple_of(row * field_cases, 8)
            column = jnp.sum(
                ring[n - 1 + t, d, pl.ds(at, field_cases)] * f0[:, pl.ds(start, width)],
                axis=0,
                keepdims=True,
            )
            g0[...] = g0[...] + fold(jnp.where(members(segment), column, 0.0))

    def gather_step(t, carry):
        step = n + t
        for h in range(SUBS):
            s0_copy(t, h).wait()
            second(t, pl.ds(0, cases), (h,))
            if h == 0:
                gradient(t)
            for d in range(2):
                ring_copy(step - 1, d, h).wait_recv()

                @pl.when(t < n - 2)
                def _():
                    ring_copy(step, d, h).start()

        return carry

    lax.fori_loop(0, n - 1, gather_step, 0)
    for d in range(2):
        s0_copy(n - 1, d).wait()
    gradient(n - 1)
    pair_grads[0] = jnp.sum(g1[...], axis=1, keepdims=True) + jnp.zeros((segments, LANES), jnp.float32)
    pair_grads[1] = jnp.sum(g0[...], axis=1, keepdims=True) + jnp.zeros((segments, LANES), jnp.float32)
    grad_copy = pair_copy(pair_grads.at[pl.ds(0, 2)], pair_grads.at[pl.ds(2, 2)], 2)
    grad_copy.start()
    second(n - 1, theirs)
    pair_copy(total.at[theirs], other, 1).start()
    grad_copy.wait_recv()
    row_grads[row] = pair_grads[pl.ds(0, 2)] + pair_grads[pl.ds(2, 2)]
    for k in range(1, n):
        row_copy(k).start()
    second(n - 1, mine)
    for k in range(1, n):
        row_arrival(k).wait_recv()
    grads = row_grads[0]
    for k in range(1, n):
        grads = grads + row_grads[k]
    g1_out[...] = flat(grads[0, :, :1]) / cases
    g0_out[...] = flat(grads[1, :, :1]) / cases
    pair_copy(total.at[theirs], other, 1).wait_recv()
    out[...] = total[mine] + other[...]

    pair_copy(own, peer, 0).wait_send()
    pair_copy(total.at[theirs], other, 1).wait_send()
    grad_copy.wait_send()
    for k in range(1, n):
        row_copy(k).wait_send()

    def drain(step, carry):
        for d in range(2):
            for h in range(SUBS):
                ring_copy(step, d, h).wait_send()
        return carry

    lax.fori_loop(0, 2 * n - 2, drain, 0)


def ring_call(n, args):
    (cot, rot, cur, ptab, ctab, seg1, gain1, f1, s1, seg0, gain0, f0, s0) = args
    local_cases, depth = cot.shape
    cases = 2 * local_cases
    columns = s1.shape[1]
    width = columns // (2 * n)
    segments = gain1.shape[0]
    vmem = pl.BlockSpec(memory_space=pltpu.VMEM)
    hbm = pl.BlockSpec(memory_space=pl.ANY)
    f32, bf16 = jnp.float32, jnp.bfloat16
    dma = pltpu.SemaphoreType.DMA
    return pl.pallas_call(
        functools.partial(ring_kernel, n),
        out_shape=(
            jax.ShapeDtypeStruct((local_cases, depth), f32),
            jax.ShapeDtypeStruct((1, segments), f32),
            jax.ShapeDtypeStruct((1, segments), f32),
        ),
        in_specs=[vmem] * 8 + [hbm] + [vmem] * 3 + [hbm],
        out_specs=(vmem, vmem, vmem),
        scratch_shapes=[
            pltpu.VMEM((local_cases, depth), f32),
            pltpu.VMEM((local_cases, depth), f32),
            pltpu.VMEM((cases, depth), bf16),
            pltpu.VMEM((cases, depth), bf16),
            pltpu.VMEM((2 * n, depth, width), f32),
            pltpu.VMEM((2 * n, width, depth), f32),
            pltpu.VMEM((2 * n - 1, 2, cases, width), f32),
            pltpu.VMEM((2, 2, cases, width), f32),
            pltpu.VMEM((cases, depth), f32),
            pltpu.VMEM((local_cases, depth), f32),
            pltpu.VMEM((segments, LANES), f32),
            pltpu.VMEM((segments, LANES), f32),
            pltpu.VMEM((4, segments, LANES), f32),
            pltpu.VMEM((n, 2, segments, LANES), f32),
            dma((2 * n - 1, 2, SUBS)),
            dma((2 * n - 1, 2, SUBS)),
            dma((2 * n,)),
            dma((2 * n,)),
            dma((3,)),
            dma((3,)),
            dma((n,)),
            dma((n,)),
        ],
        compiler_params=pltpu.CompilerParams(
            collective_id=0, has_side_effects=True, vmem_limit_bytes=62 * 1024 * 1024
        ),
        cost_estimate=pl.CostEstimate(
            flops=12 * cases * depth * columns, bytes_accessed=12 * depth * columns, transcendentals=0
        ),
    )(
        cot, rot[None, :], cur[None, :], ptab, ctab, seg1[None, :], gain1[None, :], f1, s1,
        seg0[None, :], gain0[None, :], f0, s0,
    )


def local(n, *args):
    (cot, rot, cur, ptab, ctab, seg1, gain1, f1, s1, seg0, gain0, f0, s0) = args
    width = s1.shape[1] // (2 * n)
    if n % 2 == 0 and width % LANES == 0 and width * 2 * n == s1.shape[1]:
        adjoint_zero, grad_one, grad_zero = ring_call(n, args)
        return adjoint_zero, grad_one[0], grad_zero[0]
    highest = lax.Precision.HIGHEST
    num_segments = gain1.shape[0]
    adjoint_seed = cot + lookup(rot, ptab) + lookup(cur, ctab)
    scaled_two = adjoint_seed * segment_rows(seg1, gain1)[None, :]
    partial_one = segment_total(jnp.sum(adjoint_seed * f1, axis=0), seg1, num_segments)
    all_seeds = lax.all_gather(scaled_two, "case", axis=0, tiled=True)
    total_cases = all_seeds.shape[0]
    own_adjoint = lax.psum_scatter(
        jnp.dot(all_seeds, s1, precision=highest, preferred_element_type=jnp.float32),
        "row",
        scatter_dimension=0,
        tiled=True,
    )
    scaled_one = own_adjoint * segment_rows(seg0, gain0)[None, :]
    zero_terms = jnp.dot(
        lax.all_gather(scaled_one, "row", axis=0, tiled=True),
        s0,
        precision=highest,
        preferred_element_type=jnp.float32,
    )
    partial_zero = segment_total(jnp.sum(own_adjoint * f0, axis=0), seg0, num_segments)
    adjoint_zero = lax.psum_scatter(zero_terms, "case", scatter_dimension=0, tiled=True)
    grad_one, grad_zero = lax.psum((partial_one, partial_zero), ("row", "case"))
    return (adjoint_zero, grad_one / total_cases, grad_zero / total_cases)


def solution(mesh):
    placed = (
        P(("grp", "case"), "row"),
        P(("grp", "case")),
        P(("grp", "case")),
        P("grp", "row"),
        P("grp", "row"),
        P(("grp", "row")),
        P("grp"),
        P(("grp", "case"), "row"),
        P(("grp", "row"), "case"),
        P(("grp", "case")),
        P("grp"),
        P(("grp", "row"), "case"),
        P(("grp", "case"), "row"),
    )
    return jax.shard_map(
        functools.partial(local, mesh.shape["row"]),
        mesh=mesh,
        in_specs=placed,
        out_specs=(P(("grp", "case"), "row"), P("grp"), P("grp")),
        check_vma=False,
    )
```

```python
import functools

import jax
import jax.numpy as jnp
from jax import lax
from jax.experimental import pallas as pl
from jax.experimental.pallas import tpu as pltpu
from jax.sharding import PartitionSpec as P

MESH = pl.DeviceIdType.MESH
LANES = 128
SUBS = 2


def lookup(which, lookup_table):
    onehot = (which[:, None] == jnp.arange(lookup_table.shape[0], dtype=jnp.int32)[None, :]).astype(
        jnp.float32
    )
    return jnp.dot(
        onehot, lookup_table, precision=lax.Precision.HIGHEST, preferred_element_type=jnp.float32
    )


def segment_rows(segment, gains):
    onehot = (segment[:, None] == jnp.arange(gains.shape[0], dtype=jnp.int32)[None, :]).astype(
        jnp.float32
    )
    return jnp.dot(
        onehot, gains, precision=lax.Precision.HIGHEST, preferred_element_type=jnp.float32
    )


def segment_total(values, segment, num_segments):
    onehot = (segment[:, None] == jnp.arange(num_segments, dtype=jnp.int32)[None, :]).astype(
        jnp.float32
    )
    return jnp.dot(
        values, onehot, precision=lax.Precision.HIGHEST, preferred_element_type=jnp.float32
    )


def split(x):
    high = x.astype(jnp.bfloat16)
    return high, (x - high.astype(jnp.float32)).astype(jnp.bfloat16)


def dot3(a_high, a_low, b_high, b_low):
    dot = functools.partial(jnp.dot, preferred_element_type=jnp.float32)
    return dot(a_low, b_high) + dot(a_high, b_low) + dot(a_high, b_high)


def ring_kernel(
    n, cot, rot, cur, ptab, ctab, seg1, gain1, f1, s1, seg0, gain0, f0, s0,
    out, g1_out, g0_out,
    own, peer, a_high, a_low, s1_buf, s0_buf, ring, part, total, other, g1, g0, pair_grads, row_grads,
    send_sem, recv_sem, s1_sem, s0_sem, pair_send, pair_recv, row_send, row_recv,
):
    row, case = lax.axis_index("row"), lax.axis_index("case")
    half = n // 2
    upper = lax.rem(row, 2)
    place = (row // 2) * (1 - upper) + (n - 1 - row // 2) * upper

    def row_at(position):
        position = lax.rem(position + n, n)
        far = position // half
        return (1 - far) * 2 * position + far * (2 * (n - 1 - position) + 1)

    right, left = row_at(place + 1), row_at(place - 1)
    targets = (right, left)
    local_cases = cot.shape[0]
    cases = 2 * local_cases
    width = ring.shape[3]
    sub = cases // SUBS
    field_cases = f0.shape[0]
    segments = gain1.shape[1]

    def chunk(step, d):
        c = lax.rem(place + 2 * n - step, n) if d == 0 else lax.rem(place + step, n)
        return 2 * c + d

    def second_chunk(t, d):
        return chunk(t + n - 1, d)

    def s1_copy(step, d):
        start = pl.multiple_of(chunk(step, d) * width, width)
        return pltpu.make_async_copy(
            s1.at[:, pl.ds(start, width)], s1_buf.at[2 * step + d], s1_sem.at[2 * step + d]
        )

    def s0_copy(t, d):
        start = pl.multiple_of(second_chunk(t, d) * width, width)
        return pltpu.make_async_copy(
            s0.at[pl.ds(start, width)], s0_buf.at[2 * t + d], s0_sem.at[2 * t + d]
        )

    def ring_copy(step, d, h):
        rows = pl.ds(h * sub, sub)
        return pltpu.make_async_remote_copy(
            src_ref=ring.at[step, d, rows],
            dst_ref=ring.at[step + 1, d, rows],
            send_sem=send_sem.at[step, d, h],
            recv_sem=recv_sem.at[step + 1, d, h],
            device_id={"row": targets[d]},
            device_id_type=MESH,
        )

    def pair_copy(src, dst, at):
        return pltpu.make_async_remote_copy(
            src_ref=src,
            dst_ref=dst,
            send_sem=pair_send.at[at],
            recv_sem=pair_recv.at[at],
            device_id={"case": 1 - case},
            device_id_type=MESH,
        )

    def row_copy(k):
        return pltpu.make_async_remote_copy(
            src_ref=row_grads.at[row],
            dst_ref=row_grads.at[row],
            send_sem=row_send.at[k],
            recv_sem=row_recv.at[row],
            device_id={"row": lax.rem(row + k, n)},
            device_id_type=MESH,
        )

    def row_arrival(k):
        source = lax.rem(row + k, n)
        return pltpu.make_async_remote_copy(
            src_ref=row_grads.at[source],
            dst_ref=row_grads.at[source],
            send_sem=row_send.at[k],
            recv_sem=row_recv.at[source],
            device_id={"row": source},
            device_id_type=MESH,
        )

    barrier = pltpu.get_barrier_semaphore()
    for k in range(1, n):
        pl.semaphore_signal(
            barrier, inc=1, device_id={"row": lax.rem(row + k, n)}, device_id_type=MESH
        )
    pl.semaphore_signal(barrier, inc=1, device_id={"case": 1 - case}, device_id_type=MESH)

    for step in range(n):
        for d in range(2):
            s1_copy(step, d).start()

    highest = functools.partial(
        jnp.dot, precision=lax.Precision.HIGHEST, preferred_element_type=jnp.float32
    )

    def pick(index, count):
        ids = lax.broadcasted_iota(jnp.int32, (local_cases, count), 1)
        column = upright(index.astype(jnp.float32)).astype(jnp.int32)
        return jnp.where(ids == column, 1.0, 0.0).astype(jnp.float32)

    def diagonal(size):
        down = lax.broadcasted_iota(jnp.int32, (size, size), 0)
        return down == lax.broadcasted_iota(jnp.int32, (size, size), 1)

    def upright(values):
        return jnp.sum(jnp.where(diagonal(values.shape[1]), values, 0.0), axis=1, keepdims=True)

    def flat(values):
        return jnp.sum(jnp.where(diagonal(values.shape[0]), values, 0.0), axis=0, keepdims=True)

    gains_one, gains_zero = upright(gain1[...]), upright(gain0[...])

    def members(segment):
        return lax.broadcasted_iota(jnp.int32, (segments, segment.shape[1]), 0) == segment

    def gain_row(segment, gains):
        return jnp.sum(jnp.where(members(segment), gains, 0.0), axis=0, keepdims=True)

    def fold(values):
        folded = values[:, :LANES]
        for at in range(LANES, values.shape[1], LANES):
            folded = folded + values[:, at : at + LANES]
        return folded

    seed = (
        cot[...]
        + highest(pick(rot[...], ptab.shape[0]), ptab[...])
        + highest(pick(cur[...], ctab.shape[0]), ctab[...])
    )
    own[...] = seed * gain_row(seg1[...], gains_one)
    pl.semaphore_wait(barrier, n)
    pair_copy(own, peer, 0).start()
    mine = pl.ds(pl.multiple_of(case * local_cases, local_cases), local_cases)
    theirs = pl.ds(pl.multiple_of((1 - case) * local_cases, local_cases), local_cases)
    a_high[mine], a_low[mine] = split(own[...])
    column = jnp.sum(seed * f1[...], axis=0, keepdims=True)
    g1[...] = fold(jnp.where(members(seg1[...]), column, 0.0))
    g0[...] = jnp.zeros_like(g0)
    total[...] = jnp.zeros_like(total)
    pair_copy(own, peer, 0).wait_recv()
    a_high[theirs], a_low[theirs] = split(peer[...])

    def product(step, d):
        s1_copy(step, d).wait()
        b_high, b_low = split(s1_buf[2 * step + d])
        return dot3(a_high[...], a_low[...], b_high, b_low)

    for d in range(2):
        ring[0, d] = product(0, d)
        for h in range(SUBS):
            ring_copy(0, d, h).start()
    for t in range(n):
        for d in range(2):
            s0_copy(t, d).start()

    def reduce_step(step, carry):
        now = lax.rem(step, 2)
        for h in range(SUBS):
            for d in range(2):
                rows = pl.ds(h * sub, sub)
                ring_copy(step - 1, d, h).wait_recv()
                ring[step, d, rows] = ring[step, d, rows] + part[now, d, rows]
                ring_copy(step, d, h).start()

            @pl.when(step < n - 1)
            def _():
                part[1 - now, h] = product(step + 1, h)

        return carry

    for d in range(2):
        part[1, d] = product(1, d)

    lax.fori_loop(1, n, reduce_step, 0)

    def second(t, rows, directions=(0, 1)):
        for d in directions:
            start = pl.multiple_of(second_chunk(t, d) * width, width)
            segment = seg0[:, pl.ds(start, width)]
            x_high, x_low = split(ring[n - 1 + t, d, rows] * gain_row(segment, gains_zero))
            b_high, b_low = split(s0_buf[2 * t + d])
            total[rows] = total[rows] + dot3(x_high, x_low, b_high, b_low)

    def gradient(t):
        for d in range(2):
            start = pl.multiple_of(second_chunk(t, d) * width, width)
            segment = seg0[:, pl.ds(start, width)]
            at = pl.multiple_of(row * field_cases, 8)
            column = jnp.sum(
                ring[n - 1 + t, d, pl.ds(at, field_cases)] * f0[:, pl.ds(start, width)],
                axis=0,
                keepdims=True,
            )
            g0[...] = g0[...] + fold(jnp.where(members(segment), column, 0.0))

    def gather_step(t, carry):
        step = n + t
        for h in range(SUBS):
            s0_copy(t, h).wait()
            second(t, pl.ds(0, cases), (h,))
            if h == 0:
                gradient(t)
            for d in range(2):
                ring_copy(step - 1, d, h).wait_recv()

                @pl.when(t < n - 2)
                def _():
                    ring_copy(step, d, h).start()

        return carry

    lax.fori_loop(0, n - 1, gather_step, 0)
    for d in range(2):
        s0_copy(n - 1, d).wait()
    gradient(n - 1)
    pair_grads[0] = jnp.zeros(pair_grads.shape[1:], jnp.float32)
    pair_grads[0, 0:1, :segments] = flat(jnp.sum(g1[...], axis=1, keepdims=True))
    pair_grads[0, 1:2, :segments] = flat(jnp.sum(g0[...], axis=1, keepdims=True))
    grad_copy = pair_copy(pair_grads.at[0], pair_grads.at[1], 2)
    grad_copy.start()
    second(n - 1, theirs)
    pair_copy(total.at[theirs], other, 1).start()
    grad_copy.wait_recv()
    row_grads[row] = pair_grads[0] + pair_grads[1]
    for k in range(1, n):
        row_copy(k).start()
    second(n - 1, mine)
    for k in range(1, n):
        row_arrival(k).wait_recv()
    grads = row_grads[0]
    for k in range(1, n):
        grads = grads + row_grads[k]
    g1_out[...] = grads[0:1, :segments] / cases
    g0_out[...] = grads[1:2, :segments] / cases
    pair_copy(total.at[theirs], other, 1).wait_recv()
    out[...] = total[mine] + other[...]

    pair_copy(own, peer, 0).wait_send()
    pair_copy(total.at[theirs], other, 1).wait_send()
    grad_copy.wait_send()
    for k in range(1, n):
        row_copy(k).wait_send()

    def drain(step, carry):
        for d in range(2):
            for h in range(SUBS):
                ring_copy(step, d, h).wait_send()
        return carry

    lax.fori_loop(0, 2 * n - 2, drain, 0)


def ring_call(n, args):
    (cot, rot, cur, ptab, ctab, seg1, gain1, f1, s1, seg0, gain0, f0, s0) = args
    local_cases, depth = cot.shape
    cases = 2 * local_cases
    columns = s1.shape[1]
    width = columns // (2 * n)
    segments = gain1.shape[0]
    vmem = pl.BlockSpec(memory_space=pltpu.VMEM)
    hbm = pl.BlockSpec(memory_space=pl.ANY)
    f32, bf16 = jnp.float32, jnp.bfloat16
    dma = pltpu.SemaphoreType.DMA
    return pl.pallas_call(
        functools.partial(ring_kernel, n),
        out_shape=(
            jax.ShapeDtypeStruct((local_cases, depth), f32),
            jax.ShapeDtypeStruct((1, segments), f32),
            jax.ShapeDtypeStruct((1, segments), f32),
        ),
        in_specs=[vmem] * 8 + [hbm] + [vmem] * 3 + [hbm],
        out_specs=(vmem, vmem, vmem),
        scratch_shapes=[
            pltpu.VMEM((local_cases, depth), f32),
            pltpu.VMEM((local_cases, depth), f32),
            pltpu.VMEM((cases, depth), bf16),
            pltpu.VMEM((cases, depth), bf16),
            pltpu.VMEM((2 * n, depth, width), f32),
            pltpu.VMEM((2 * n, width, depth), f32),
            pltpu.VMEM((2 * n - 1, 2, cases, width), f32),
            pltpu.VMEM((2, 2, cases, width), f32),
            pltpu.VMEM((cases, depth), f32),
            pltpu.VMEM((local_cases, depth), f32),
            pltpu.VMEM((segments, LANES), f32),
            pltpu.VMEM((segments, LANES), f32),
            pltpu.VMEM((2, 8, pl.cdiv(segments, LANES) * LANES), f32),
            pltpu.VMEM((n, 8, pl.cdiv(segments, LANES) * LANES), f32),
            dma((2 * n - 1, 2, SUBS)),
            dma((2 * n - 1, 2, SUBS)),
            dma((2 * n,)),
            dma((2 * n,)),
            dma((3,)),
            dma((3,)),
            dma((n,)),
            dma((n,)),
        ],
        compiler_params=pltpu.CompilerParams(
            collective_id=0, has_side_effects=True, vmem_limit_bytes=62 * 1024 * 1024
        ),
        cost_estimate=pl.CostEstimate(
            flops=12 * cases * depth * columns, bytes_accessed=12 * depth * columns, transcendentals=0
        ),
    )(
        cot, rot[None, :], cur[None, :], ptab, ctab, seg1[None, :], gain1[None, :], f1, s1,
        seg0[None, :], gain0[None, :], f0, s0,
    )


def local(n, *args):
    (cot, rot, cur, ptab, ctab, seg1, gain1, f1, s1, seg0, gain0, f0, s0) = args
    width = s1.shape[1] // (2 * n)
    if n % 2 == 0 and width % LANES == 0 and width * 2 * n == s1.shape[1]:
        adjoint_zero, grad_one, grad_zero = ring_call(n, args)
        return adjoint_zero, grad_one[0], grad_zero[0]
    highest = lax.Precision.HIGHEST
    num_segments = gain1.shape[0]
    adjoint_seed = cot + lookup(rot, ptab) + lookup(cur, ctab)
    scaled_two = adjoint_seed * segment_rows(seg1, gain1)[None, :]
    partial_one = segment_total(jnp.sum(adjoint_seed * f1, axis=0), seg1, num_segments)
    all_seeds = lax.all_gather(scaled_two, "case", axis=0, tiled=True)
    total_cases = all_seeds.shape[0]
    own_adjoint = lax.psum_scatter(
        jnp.dot(all_seeds, s1, precision=highest, preferred_element_type=jnp.float32),
        "row",
        scatter_dimension=0,
        tiled=True,
    )
    scaled_one = own_adjoint * segment_rows(seg0, gain0)[None, :]
    zero_terms = jnp.dot(
        lax.all_gather(scaled_one, "row", axis=0, tiled=True),
        s0,
        precision=highest,
        preferred_element_type=jnp.float32,
    )
    partial_zero = segment_total(jnp.sum(own_adjoint * f0, axis=0), seg0, num_segments)
    adjoint_zero = lax.psum_scatter(zero_terms, "case", scatter_dimension=0, tiled=True)
    grad_one, grad_zero = lax.psum((partial_one, partial_zero), ("row", "case"))
    return (adjoint_zero, grad_one / total_cases, grad_zero / total_cases)


def solution(mesh):
    placed = (
        P(("grp", "case"), "row"),
        P(("grp", "case")),
        P(("grp", "case")),
        P("grp", "row"),
        P("grp", "row"),
        P(("grp", "row")),
        P("grp"),
        P(("grp", "case"), "row"),
        P(("grp", "row"), "case"),
        P(("grp", "case")),
        P("grp"),
        P(("grp", "row"), "case"),
        P(("grp", "case"), "row"),
    )
    return jax.shard_map(
        functools.partial(local, mesh.shape["row"]),
        mesh=mesh,
        in_specs=placed,
        out_specs=(P(("grp", "case"), "row"), P("grp"), P("grp")),
        check_vma=False,
    )
```

```python
import functools

import jax
import jax.numpy as jnp
from jax import lax
from jax.experimental import pallas as pl
from jax.experimental.pallas import tpu as pltpu
from jax.sharding import PartitionSpec as P

MESH = pl.DeviceIdType.MESH
LANES = 128
SUBS = 2


def lookup(which, lookup_table):
    onehot = (which[:, None] == jnp.arange(lookup_table.shape[0], dtype=jnp.int32)[None, :]).astype(
        jnp.float32
    )
    return jnp.dot(
        onehot, lookup_table, precision=lax.Precision.HIGHEST, preferred_element_type=jnp.float32
    )


def segment_rows(segment, gains):
    onehot = (segment[:, None] == jnp.arange(gains.shape[0], dtype=jnp.int32)[None, :]).astype(
        jnp.float32
    )
    return jnp.dot(
        onehot, gains, precision=lax.Precision.HIGHEST, preferred_element_type=jnp.float32
    )


def segment_total(values, segment, num_segments):
    onehot = (segment[:, None] == jnp.arange(num_segments, dtype=jnp.int32)[None, :]).astype(
        jnp.float32
    )
    return jnp.dot(
        values, onehot, precision=lax.Precision.HIGHEST, preferred_element_type=jnp.float32
    )


def split(x):
    high = x.astype(jnp.bfloat16)
    return high, (x - high.astype(jnp.float32)).astype(jnp.bfloat16)


def dot3(a_high, a_low, b_high, b_low):
    dot = functools.partial(jnp.dot, preferred_element_type=jnp.float32)
    return dot(a_low, b_high) + dot(a_high, b_low) + dot(a_high, b_high)


def ring_kernel(
    n, cot, rot, cur, ptab, ctab, seg1, gain1, f1, s1, seg0, gain0, f0, s0,
    out, g1_out, g0_out,
    own, peer, a_high, a_low, s1_buf, s0_buf, ring, part, total, other, g1, g0, pair_grads, row_grads,
    send_sem, recv_sem, s1_sem, s0_sem, pair_send, pair_recv, row_send, row_recv,
):
    row, case = lax.axis_index("row"), lax.axis_index("case")
    half = n // 2
    upper = lax.rem(row, 2)
    place = (row // 2) * (1 - upper) + (n - 1 - row // 2) * upper

    def row_at(position):
        position = lax.rem(position + n, n)
        far = position // half
        return (1 - far) * 2 * position + far * (2 * (n - 1 - position) + 1)

    right, left = row_at(place + 1), row_at(place - 1)
    targets = (right, left)
    local_cases = cot.shape[0]
    cases = 2 * local_cases
    width = ring.shape[3]
    sub = cases // SUBS
    field_cases = f0.shape[0]
    segments = gain1.shape[1]

    def chunk(step, d):
        c = lax.rem(place + 2 * n - step, n) if d == 0 else lax.rem(place + step, n)
        return 2 * c + d

    def second_chunk(t, d):
        return chunk(t + n - 1, d)

    def s1_copy(step, d):
        start = pl.multiple_of(chunk(step, d) * width, width)
        return pltpu.make_async_copy(
            s1.at[:, pl.ds(start, width)], s1_buf.at[2 * step + d], s1_sem.at[2 * step + d]
        )

    def s0_copy(t, d):
        start = pl.multiple_of(second_chunk(t, d) * width, width)
        return pltpu.make_async_copy(
            s0.at[pl.ds(start, width)], s0_buf.at[2 * t + d], s0_sem.at[2 * t + d]
        )

    def ring_copy(step, d, h):
        rows = pl.ds(h * sub, sub)
        return pltpu.make_async_remote_copy(
            src_ref=ring.at[step, d, rows],
            dst_ref=ring.at[step + 1, d, rows],
            send_sem=send_sem.at[step, d, h],
            recv_sem=recv_sem.at[step + 1, d, h],
            device_id={"row": targets[d]},
            device_id_type=MESH,
        )

    def pair_copy(src, dst, at):
        return pltpu.make_async_remote_copy(
            src_ref=src,
            dst_ref=dst,
            send_sem=pair_send.at[at],
            recv_sem=pair_recv.at[at],
            device_id={"case": 1 - case},
            device_id_type=MESH,
        )

    def row_copy(k):
        return pltpu.make_async_remote_copy(
            src_ref=row_grads.at[row],
            dst_ref=row_grads.at[row],
            send_sem=row_send.at[k],
            recv_sem=row_recv.at[row],
            device_id={"row": lax.rem(row + k, n)},
            device_id_type=MESH,
        )

    def row_arrival(k):
        source = lax.rem(row + k, n)
        return pltpu.make_async_remote_copy(
            src_ref=row_grads.at[source],
            dst_ref=row_grads.at[source],
            send_sem=row_send.at[k],
            recv_sem=row_recv.at[source],
            device_id={"row": source},
            device_id_type=MESH,
        )

    barrier = pltpu.get_barrier_semaphore()
    for k in range(1, n):
        pl.semaphore_signal(
            barrier, inc=1, device_id={"row": lax.rem(row + k, n)}, device_id_type=MESH
        )
    pl.semaphore_signal(barrier, inc=1, device_id={"case": 1 - case}, device_id_type=MESH)

    for step in range(n):
        for d in range(2):
            s1_copy(step, d).start()

    highest = functools.partial(
        jnp.dot, precision=lax.Precision.HIGHEST, preferred_element_type=jnp.float32
    )

    def pick(index, count):
        ids = lax.broadcasted_iota(jnp.int32, (local_cases, count), 1)
        column = upright(index.astype(jnp.float32)).astype(jnp.int32)
        return jnp.where(ids == column, 1.0, 0.0).astype(jnp.float32)

    def diagonal(size):
        down = lax.broadcasted_iota(jnp.int32, (size, size), 0)
        return down == lax.broadcasted_iota(jnp.int32, (size, size), 1)

    def upright(values):
        return jnp.sum(jnp.where(diagonal(values.shape[1]), values, 0.0), axis=1, keepdims=True)

    def flat(values):
        return jnp.sum(jnp.where(diagonal(values.shape[0]), values, 0.0), axis=0, keepdims=True)

    gains_one, gains_zero = upright(gain1[...]), upright(gain0[...])

    def members(segment):
        return lax.broadcasted_iota(jnp.int32, (segments, segment.shape[1]), 0) == segment

    def gain_row(segment, gains):
        return jnp.sum(jnp.where(members(segment), gains, 0.0), axis=0, keepdims=True)

    def fold(values):
        folded = values[:, :LANES]
        for at in range(LANES, values.shape[1], LANES):
            folded = folded + values[:, at : at + LANES]
        return folded

    seed = (
        cot[...]
        + highest(pick(rot[...], ptab.shape[0]), ptab[...])
        + highest(pick(cur[...], ctab.shape[0]), ctab[...])
    )
    own[...] = seed * gain_row(seg1[...], gains_one)
    pl.semaphore_wait(barrier, n)
    pair_copy(own, peer, 0).start()
    mine = pl.ds(pl.multiple_of(case * local_cases, local_cases), local_cases)
    theirs = pl.ds(pl.multiple_of((1 - case) * local_cases, local_cases), local_cases)
    a_high[mine], a_low[mine] = split(own[...])
    column = jnp.sum(seed * f1[...], axis=0, keepdims=True)
    g1[...] = fold(jnp.where(members(seg1[...]), column, 0.0))
    g0[...] = jnp.zeros_like(g0)
    total[...] = jnp.zeros_like(total)
    pair_copy(own, peer, 0).wait_recv()
    a_high[theirs], a_low[theirs] = split(peer[...])

    def product(step, d):
        s1_copy(step, d).wait()
        b_high, b_low = split(s1_buf[2 * step + d])
        return dot3(a_high[...], a_low[...], b_high, b_low)

    for d in range(2):
        ring[0, d] = product(0, d)
        for h in range(SUBS):
            ring_copy(0, d, h).start()
    for t in range(n):
        for d in range(2):
            s0_copy(t, d).start()

    def reduce_step(step, carry):
        for d in range(2):
            part[d] = product(step, d)
        for h in range(SUBS):
            for d in range(2):
                rows = pl.ds(h * sub, sub)
                ring_copy(step - 1, d, h).wait_recv()
                ring[step, d, rows] = ring[step, d, rows] + part[d, rows]
                ring_copy(step, d, h).start()
        return carry

    lax.fori_loop(1, n, reduce_step, 0)

    def second(t, rows):
        for d in range(2):
            start = pl.multiple_of(second_chunk(t, d) * width, width)
            segment = seg0[:, pl.ds(start, width)]
            x_high, x_low = split(ring[n - 1 + t, d, rows] * gain_row(segment, gains_zero))
            b_high, b_low = split(s0_buf[2 * t + d])
            total[rows] = total[rows] + dot3(x_high, x_low, b_high, b_low)

    def gradient(t):
        for d in range(2):
            start = pl.multiple_of(second_chunk(t, d) * width, width)
            segment = seg0[:, pl.ds(start, width)]
            at = pl.multiple_of(row * field_cases, 8)
            column = jnp.sum(
                ring[n - 1 + t, d, pl.ds(at, field_cases)] * f0[:, pl.ds(start, width)],
                axis=0,
                keepdims=True,
            )
            g0[...] = g0[...] + fold(jnp.where(members(segment), column, 0.0))

    def gather_step(t, carry):
        for d in range(2):
            s0_copy(t, d).wait()
        second(t, pl.ds(0, cases))
        gradient(t)
        step = n + t
        for h in range(SUBS):
            for d in range(2):
                ring_copy(step - 1, d, h).wait_recv()

                @pl.when(t < n - 2)
                def _():
                    ring_copy(step, d, h).start()

        return carry

    lax.fori_loop(0, n - 1, gather_step, 0)
    for d in range(2):
        s0_copy(n - 1, d).wait()
    gradient(n - 1)
    pair_grads[0] = jnp.zeros(pair_grads.shape[1:], jnp.float32)
    pair_grads[0, 0:1, :segments] = flat(jnp.sum(g1[...], axis=1, keepdims=True))
    pair_grads[0, 1:2, :segments] = flat(jnp.sum(g0[...], axis=1, keepdims=True))
    grad_copy = pair_copy(pair_grads.at[0], pair_grads.at[1], 2)
    grad_copy.start()
    second(n - 1, theirs)
    pair_copy(total.at[theirs], other, 1).start()
    grad_copy.wait_recv()
    row_grads[row] = pair_grads[0] + pair_grads[1]
    for k in range(1, n):
        row_copy(k).start()
    second(n - 1, mine)
    for k in range(1, n):
        row_arrival(k).wait_recv()
    grads = row_grads[0]
    for k in range(1, n):
        grads = grads + row_grads[k]
    g1_out[...] = grads[0:1, :segments] / cases
    g0_out[...] = grads[1:2, :segments] / cases
    pair_copy(total.at[theirs], other, 1).wait_recv()
    out[...] = total[mine] + other[...]

    pair_copy(own, peer, 0).wait_send()
    pair_copy(total.at[theirs], other, 1).wait_send()
    grad_copy.wait_send()
    for k in range(1, n):
        row_copy(k).wait_send()

    def drain(step, carry):
        for d in range(2):
            for h in range(SUBS):
                ring_copy(step, d, h).wait_send()
        return carry

    lax.fori_loop(0, 2 * n - 2, drain, 0)


def ring_call(n, args):
    (cot, rot, cur, ptab, ctab, seg1, gain1, f1, s1, seg0, gain0, f0, s0) = args
    local_cases, depth = cot.shape
    cases = 2 * local_cases
    columns = s1.shape[1]
    width = columns // (2 * n)
    segments = gain1.shape[0]
    vmem = pl.BlockSpec(memory_space=pltpu.VMEM)
    hbm = pl.BlockSpec(memory_space=pl.ANY)
    f32, bf16 = jnp.float32, jnp.bfloat16
    dma = pltpu.SemaphoreType.DMA
    return pl.pallas_call(
        functools.partial(ring_kernel, n),
        out_shape=(
            jax.ShapeDtypeStruct((local_cases, depth), f32),
            jax.ShapeDtypeStruct((1, segments), f32),
            jax.ShapeDtypeStruct((1, segments), f32),
        ),
        in_specs=[vmem] * 8 + [hbm] + [vmem] * 3 + [hbm],
        out_specs=(vmem, vmem, vmem),
        scratch_shapes=[
            pltpu.VMEM((local_cases, depth), f32),
            pltpu.VMEM((local_cases, depth), f32),
            pltpu.VMEM((cases, depth), bf16),
            pltpu.VMEM((cases, depth), bf16),
            pltpu.VMEM((2 * n, depth, width), f32),
            pltpu.VMEM((2 * n, width, depth), f32),
            pltpu.VMEM((2 * n - 1, 2, cases, width), f32),
            pltpu.VMEM((2, cases, width), f32),
            pltpu.VMEM((cases, depth), f32),
            pltpu.VMEM((local_cases, depth), f32),
            pltpu.VMEM((segments, LANES), f32),
            pltpu.VMEM((segments, LANES), f32),
            pltpu.VMEM((2, 8, pl.cdiv(segments, LANES) * LANES), f32),
            pltpu.VMEM((n, 8, pl.cdiv(segments, LANES) * LANES), f32),
            dma((2 * n - 1, 2, SUBS)),
            dma((2 * n - 1, 2, SUBS)),
            dma((2 * n,)),
            dma((2 * n,)),
            dma((3,)),
            dma((3,)),
            dma((n,)),
            dma((n,)),
        ],
        compiler_params=pltpu.CompilerParams(
            collective_id=0, has_side_effects=True, vmem_limit_bytes=62 * 1024 * 1024
        ),
        cost_estimate=pl.CostEstimate(
            flops=12 * cases * depth * columns, bytes_accessed=12 * depth * columns, transcendentals=0
        ),
    )(
        cot, rot[None, :], cur[None, :], ptab, ctab, seg1[None, :], gain1[None, :], f1, s1,
        seg0[None, :], gain0[None, :], f0, s0,
    )


def local(n, *args):
    (cot, rot, cur, ptab, ctab, seg1, gain1, f1, s1, seg0, gain0, f0, s0) = args
    width = s1.shape[1] // (2 * n)
    if n % 2 == 0 and width % LANES == 0 and width * 2 * n == s1.shape[1]:
        adjoint_zero, grad_one, grad_zero = ring_call(n, args)
        return adjoint_zero, grad_one[0], grad_zero[0]
    highest = lax.Precision.HIGHEST
    num_segments = gain1.shape[0]
    adjoint_seed = cot + lookup(rot, ptab) + lookup(cur, ctab)
    scaled_two = adjoint_seed * segment_rows(seg1, gain1)[None, :]
    partial_one = segment_total(jnp.sum(adjoint_seed * f1, axis=0), seg1, num_segments)
    all_seeds = lax.all_gather(scaled_two, "case", axis=0, tiled=True)
    total_cases = all_seeds.shape[0]
    own_adjoint = lax.psum_scatter(
        jnp.dot(all_seeds, s1, precision=highest, preferred_element_type=jnp.float32),
        "row",
        scatter_dimension=0,
        tiled=True,
    )
    scaled_one = own_adjoint * segment_rows(seg0, gain0)[None, :]
    zero_terms = jnp.dot(
        lax.all_gather(scaled_one, "row", axis=0, tiled=True),
        s0,
        precision=highest,
        preferred_element_type=jnp.float32,
    )
    partial_zero = segment_total(jnp.sum(own_adjoint * f0, axis=0), seg0, num_segments)
    adjoint_zero = lax.psum_scatter(zero_terms, "case", scatter_dimension=0, tiled=True)
    grad_one, grad_zero = lax.psum((partial_one, partial_zero), ("row", "case"))
    return (adjoint_zero, grad_one / total_cases, grad_zero / total_cases)


def solution(mesh):
    placed = (
        P(("grp", "case"), "row"),
        P(("grp", "case")),
        P(("grp", "case")),
        P("grp", "row"),
        P("grp", "row"),
        P(("grp", "row")),
        P("grp"),
        P(("grp", "case"), "row"),
        P(("grp", "row"), "case"),
        P(("grp", "case")),
        P("grp"),
        P(("grp", "row"), "case"),
        P(("grp", "case"), "row"),
    )
    return jax.shard_map(
        functools.partial(local, mesh.shape["row"]),
        mesh=mesh,
        in_specs=placed,
        out_specs=(P(("grp", "case"), "row"), P("grp"), P("grp")),
        check_vma=False,
    )
```
